32 devices in a mesh: grp: 2 (over x), row: 8 (over z, y), col: 2 (over core).
Axes of the slice: x: 2, y: 2, z: 4, core: 2. Of those that a mesh axis runs over, the one named last changes fastest.
Arguments:
- pair: float32 [1024, 512, 128], P(('grp', 'row'), 'col'), parts along dimension 0, may hold values from -400 to 400
- token_count: int32 [2], P('grp'), parts along dimension 0, may hold values from 256 to 512
- chain_ids: int32 [1024], P('grp'), parts along dimension 0, may hold values from 0 to 5, never falling along the last dimension, each value on 1 to 170 neighbouring positions
- chain_term: float32 [128], replicated, may hold values from -4 to 4
- in_gain: float32 [2, 128], replicated, may hold values from 0.25 to 1.75
- in_bias: float32 [2, 128], replicated, may hold values from -3 to 3
- proj: bfloat16 [2, 128, 512], replicated, may hold values from -0.5 to 0.5
- gate_w: bfloat16 [2, 128, 128], replicated, may hold values from -0.5 to 0.5
- hid_gain: float32 [2, 128], replicated, may hold values from 0.25 to 1.75
- hid_bias: float32 [2, 128], replicated, may hold values from -3 to 3
- out_w: bfloat16 [2, 128, 128], replicated, may hold values from -0.5 to 0.5
Outputs:
- pair_out: float32 [1024, 512, 128], P(('grp', 'row'), 'col'), parts along dimension 0
The draws below stay inside these ranges and needn't reach their ends.
There are 2 independent parts, one for each index of `grp`. The reference program is written for one: setup_inputs(seed, part) draws one part's arguments, and reference() takes and returns one part's arrays. A program takes and returns all parts, laid end to end along the dimension named above; an argument that names none is the same for every part. Nothing has to cross between parts.
Inputs may be any that keep to these rules, and one draw needn't show every extreme that they name: `token_count`: tokens at positions below the count are real, the rest are padding. `chain_ids`: chain numbers never fall along the tokens.
All inputs are finite; a program needn't handle non-finite values.
Results may differ from the reference program's by a relative error of at most 0.0011.
Values may be sent and summed in bfloat16 or wider, within the bound.
A program may use at most 192 MiB of HBM per device.

```python
import math
import jax
import jax.numpy as jnp
import numpy as np
from jax import lax

C = 128
H = 128
N = 512


def draw_pair(key, part):
    key = jax.random.fold_in(key, 11)
    subkeys = jax.random.split(key, 4)
    channel_scale = jnp.exp(jax.random.uniform(subkeys[0], (C,), jnp.float32, -1.15, 1.15))
    row_scale = jnp.exp(jax.random.uniform(subkeys[1], (N, 1, 1), jnp.float32, -1.15, 1.15))
    col_scale = jnp.exp(jax.random.uniform(subkeys[2], (1, N, 1), jnp.float32, -1.15, 1.15))
    raw_values = jax.random.normal(subkeys[3], (N, N, C), jnp.float32)
    return raw_values * row_scale * col_scale * channel_scale


def length_profile(amount, total, most, lean):
    loads = [(1 << 20) // math.isqrt(standing ** lean) + 1 for standing in range(2, amount + 1)]
    surplus, counts = total - most - (amount - 1), [1] * (amount - 1)
    while surplus > 0:
        candidates = [i for i in range(amount - 1) if counts[i] < most]
        mass, left = sum([loads[i] for i in candidates]), surplus
        for i in candidates:
            addition = min(most - counts[i], max(1, left * loads[i] // mass), surplus)
            counts[i] = counts[i] + addition
            surplus = surplus - addition
    return np.array([most] + counts)


def uneven_parts(key, number_of, total, most, skew):
    if number_of == 2:
        one = jax.random.randint(key, (), max(1, total - most), min(most, total - 1) + 1)
        return jnp.stack([one, total - one])
    tallies = jnp.asarray(length_profile(number_of, total, most, skew), jnp.int32)
    couples = (number_of - 1) // 2
    source_of, receiver = tallies[1:1 + 2 * couples:2], tallies[2:2 + 2 * couples:2]
    slack = jnp.minimum(source_of - 1, most - receiver)
    passed = jax.random.randint(jax.random.fold_in(key, 1), (couples,), 0, 1 << 20) % (slack + 1)
    tallies = tallies.at[1:1 + 2 * couples:2].set(source_of - passed).at[2:2 + 2 * couples:2].set(receiver + passed)
    return tallies[jax.random.permutation(jax.random.fold_in(key, 2), number_of)]


def centred(rng, dims, spread, reach, kind=jnp.bfloat16):
    values = jax.random.normal(rng, dims, jnp.float32) * spread
    return jnp.minimum(jnp.maximum(values, -reach), reach).astype(kind)


def setup_inputs(seed: int = 0, part: int = 0) -> dict:
    key_of = jax.random.split(jax.random.key(seed), 12)
    part_keys = jax.random.split(jax.random.fold_in(key_of[11], part), 12)
    pair = draw_pair(jax.random.fold_in(jax.random.fold_in(key_of[11], part), 71), part)
    token_count = jax.random.randint(part_keys[1], (1,), N // 2, N + 1).astype(jnp.int32)
    chain_ids = jnp.searchsorted(jnp.cumsum(uneven_parts(part_keys[2], 6, N, N // 3, 2)), jnp.arange(N), side="right").astype(jnp.int32)
    chain_term = centred(key_of[3], (C,), 1.0, 4.0, jnp.float32)
    in_gain = jnp.clip(1.0 + 0.15 * jax.random.normal(key_of[4], (2, C), jnp.float32), 0.25, 1.75)
    in_bias = centred(key_of[5], (2, C), 0.3, 3.0, jnp.float32)
    proj = centred(key_of[6], (2, C, 4 * H), C ** -0.5, 0.5)
    gate_w = centred(key_of[7], (2, C, C), C ** -0.5, 0.5)
    hid_gain = jnp.clip(1.0 + 0.15 * jax.random.normal(key_of[8], (2, H), jnp.float32), 0.25, 1.75)
    hid_bias = centred(key_of[9], (2, H), 0.3, 3.0, jnp.float32)
    out_w = centred(key_of[10], (2, H, C), H ** -0.5, 0.5)
    return {"pair": pair, "token_count": token_count, "chain_ids": chain_ids, "chain_term": chain_term, "in_gain": in_gain, "in_bias": in_bias, "proj": proj, "gate_w": gate_w, "hid_gain": hid_gain, "hid_bias": hid_bias, "out_w": out_w}


EPSILON = 1e-05

def norm_last(values, gain, bias):
    center = values - lax.optimization_barrier(jnp.mean(values, axis=-1, keepdims=True))
    variance = lax.optimization_barrier(jnp.mean(center * center, axis=-1, keepdims=True))
    return center * lax.rsqrt(variance + EPSILON) * gain + bias

def norm_first(values, gain, bias):
    center = values - lax.optimization_barrier(jnp.mean(values, axis=0, keepdims=True))
    variance = lax.optimization_barrier(jnp.mean(center * center, axis=0, keepdims=True))
    return center * lax.rsqrt(variance + EPSILON) * gain[:, None, None] + bias[:, None, None]

def outgoing_one(operands):
    return jnp.dot(operands[0], operands[1].T, preferred_element_type=jnp.float32).astype(jnp.bfloat16)

def incoming_one(operands):
    return jnp.dot(operands[0].T, operands[1], preferred_element_type=jnp.float32).astype(jnp.bfloat16)

def reference(pair, token_count, chain_ids, chain_term, in_gain, in_bias, proj, gate_w, hid_gain, hid_bias, out_w):
    positions = jnp.arange(N, dtype=jnp.int32)
    token_valid = (positions < token_count[0]).astype(jnp.float32)
    same_chain = (chain_ids[:, None] == chain_ids[None, :]).astype(jnp.float32)
    state = pair + same_chain[:, :, None] * chain_term
    for layer_index in range(2):
        normed = norm_last(state, in_gain[layer_index], in_bias[layer_index]).astype(jnp.bfloat16)
        weights = proj[layer_index].astype(jnp.float32)

        def one_block(block_start, normed=normed, weights=weights):
            row_block = lax.dynamic_slice_in_dim(normed, block_start, 64, 0).astype(jnp.float32)
            hidden_all = jnp.einsum('ijc,cf->fij', row_block, weights)
            row_valid = lax.dynamic_slice_in_dim(token_valid, block_start, 64, 0)
            pair_mask = row_valid[:, None] * token_valid[None, :]
            left_side = (pair_mask * jax.nn.sigmoid(hidden_all[:H]) * hidden_all[H:2 * H]).astype(jnp.bfloat16)
            right_side = (pair_mask * jax.nn.sigmoid(hidden_all[2 * H:3 * H]) * hidden_all[3 * H:]).astype(jnp.bfloat16)
            return (left_side, right_side)
        starts = jnp.arange(N // 64, dtype=jnp.int32) * 64
        left_side, right_side = lax.map(one_block, starts)
        left_side = left_side.transpose(1, 0, 2, 3).reshape(H, N, N)
        right_side = right_side.transpose(1, 0, 2, 3).reshape(H, N, N)
        gate_value = jax.nn.sigmoid(jnp.einsum('ijc,cd->ijd', normed.astype(jnp.float32), gate_w[layer_index].astype(jnp.float32)))
        if layer_index == 0:
            mixed = lax.map(outgoing_one, (left_side, right_side))
        else:
            mixed = lax.map(incoming_one, (left_side, right_side))
        normed_mix = norm_first(mixed.astype(jnp.float32), hid_gain[layer_index], hid_bias[layer_index]).astype(jnp.bfloat16)
        update = jnp.einsum('hij,hc->ijc', normed_mix.astype(jnp.float32), out_w[layer_index].astype(jnp.float32))
        state = state + gate_value * update
    return state
```

```python
import functools

import jax
import jax.numpy as jnp
from jax import lax
from jax.experimental import pallas as pl
from jax.experimental.pallas import tpu as pltpu
from jax.sharding import PartitionSpec as P

EPSILON = 1e-05
VMEM_LIMIT = 56 * 1024 * 1024


def norm(values, gain, bias, axis):
    center = values - jnp.mean(values, axis=axis, keepdims=True)
    variance = jnp.mean(center * center, axis=axis, keepdims=True)
    return center * lax.rsqrt(variance + EPSILON) * gain + bias


def dot(a, b, dims):
    return lax.dot_general(a, b, (dims, ((), ())), preferred_element_type=jnp.float32)


def project_row(row, normed, row_real, col_real, proj_t, left_rows, right_rows):
    hidden = left_rows.shape[1]
    mask = row_real * col_real
    both = dot(proj_t[...], normed, ((1,), (1,)))
    left = mask * jax.nn.sigmoid(both[:hidden]) * both[hidden : 2 * hidden]
    right = mask * jax.nn.sigmoid(both[2 * hidden : 3 * hidden]) * both[3 * hidden :]
    left_rows[row] = left.astype(jnp.bfloat16)
    right_rows[row] = right.astype(jnp.bfloat16)


def add_chain(pair_row, row_chain, col_chain, chain_term):
    same = (col_chain[...] == row_chain).astype(jnp.float32)
    return pair_row + same * chain_term[...]


def update_row(state, mixed, gain, bias, gate_w, hid_gain, hid_bias, out_w):
    normed = norm(state, gain, bias, -1).astype(jnp.bfloat16)
    gate = jax.nn.sigmoid(dot(normed, gate_w, ((1,), (0,))))
    normed_mix = norm(mixed.astype(jnp.float32), hid_gain, hid_bias, 0).astype(jnp.bfloat16)
    return state + gate * dot(normed_mix, out_w, ((0,), (0,)))


def first_kernel(
    chain_s, real_s, pair, col_chain, col_real, chain_term, gain, bias, proj_t,
    left, right, left_rows, right_rows,
):
    rows = pair.shape[0]
    base = pl.program_id(0) * rows

    @pl.loop(0, rows)
    def _(row):
        state = add_chain(pair[row], chain_s[base + row], col_chain, chain_term)
        normed = norm(state, gain[0:1], bias[0:1], -1).astype(jnp.bfloat16)
        project_row(row, normed, real_s[base + row], col_real[...], proj_t, left_rows, right_rows)

    left[...] = jnp.swapaxes(left_rows[...], 0, 1)
    right[...] = jnp.swapaxes(right_rows[...], 0, 1)


def middle_kernel(
    chain_s, real_s, pair, mixed, col_chain, col_real, chain_term, gain, bias, proj_t,
    gate_w, hid_gain, hid_bias, out_w,
    state_out, left, right, left_rows, right_rows, mixed_rows,
):
    rows = pair.shape[0]
    base = pl.program_id(0) * rows
    mixed_rows[...] = jnp.swapaxes(mixed[...], 0, 1)

    @pl.loop(0, rows)
    def _(row):
        state = add_chain(pair[row], chain_s[base + row], col_chain, chain_term)
        state = update_row(
            state, mixed_rows[row], gain[0:1], bias[0:1], gate_w[...], hid_gain[...],
            hid_bias[...], out_w[...],
        )
        state_out[row] = state
        normed = norm(state, gain[1:2], bias[1:2], -1).astype(jnp.bfloat16)
        project_row(row, normed, real_s[base + row], col_real[...], proj_t, left_rows, right_rows)

    left[...] = jnp.swapaxes(left_rows[...], 0, 1)
    right[...] = jnp.swapaxes(right_rows[...], 0, 1)


def last_kernel(
    state_in, mixed, gain, bias, gate_w, hid_gain, hid_bias, out_w, state_out, mixed_rows
):
    rows = state_in.shape[0]
    mixed_rows[...] = jnp.swapaxes(mixed[...], 0, 1)

    @pl.loop(0, rows)
    def _(row):
        state_out[row] = update_row(
            state_in[row], mixed_rows[row], gain[1:2], bias[1:2], gate_w[...], hid_gain[...],
            hid_bias[...], out_w[...],
        )


def triangle_kernel(outgoing, col_count, left, right, mixed):
    blocks, _, rows_here, cols_here = left.shape
    row_count = blocks // col_count
    tokens = row_count * rows_here

    def part(ref, c):
        value = ref[...].reshape(row_count, col_count, rows_here, cols_here)[:, c]
        return value.reshape(tokens, cols_here)

    if outgoing:
        total = None
        for c in range(col_count):
            term = dot(part(left, c), part(right, c), ((1,), (1,)))
            total = term if total is None else total + term
        total = total.astype(jnp.bfloat16)
        for c in range(col_count):
            piece = total[:, c * cols_here : (c + 1) * cols_here]
            piece = piece.reshape(row_count, rows_here, cols_here)
            for r in range(row_count):
                mixed[r * col_count + c, 0] = piece[r]
    else:
        for ci in range(col_count):
            for cj in range(col_count):
                total = dot(part(left, ci), part(right, cj), ((0,), (0,))).astype(jnp.bfloat16)
                span = cols_here // rows_here
                for r in range(span):
                    mixed[(ci * span + r) * col_count + cj, 0] = total[
                        r * rows_here : (r + 1) * rows_here
                    ]


def triangle(left, right, outgoing):
    hidden, rows_here, cols_here = left.shape
    row_count = lax.axis_size("row")
    col_count = lax.axis_size("col")
    blocks = row_count * col_count
    per_device = hidden // blocks
    recv = []
    for side in (left, right):
        side = side.reshape(blocks, per_device, rows_here, cols_here)
        recv.append(lax.all_to_all(side, ("row", "col"), 0, 0, tiled=True))
    spec = pl.BlockSpec((blocks, 1, rows_here, cols_here), lambda h: (0, h, 0, 0))
    mixed = pl.pallas_call(
        functools.partial(triangle_kernel, outgoing, col_count),
        grid=(per_device,),
        in_specs=[spec, spec],
        out_specs=spec,
        out_shape=jax.ShapeDtypeStruct(recv[0].shape, jnp.bfloat16),
        compiler_params=pltpu.CompilerParams(vmem_limit_bytes=VMEM_LIMIT),
        name="triangle_product",
    )(*recv)
    mixed = lax.all_to_all(mixed, ("row", "col"), 0, 0, tiled=True)
    return mixed.reshape(hidden, rows_here, cols_here)


def body(
    pair, token_count, chain_ids, chain_term, in_gain, in_bias, proj, gate_w, hid_gain,
    hid_bias, out_w,
):
    rows_here, cols_here, width = pair.shape
    hidden = proj.shape[2] // 4
    row_first = lax.axis_index("row") * rows_here
    col_first = lax.axis_index("col") * cols_here
    positions = jnp.arange(chain_ids.shape[0], dtype=jnp.int32)
    real = (positions < token_count[0]).astype(jnp.float32)
    row_real = lax.dynamic_slice_in_dim(real, row_first, rows_here, 0)
    col_real = lax.dynamic_slice_in_dim(real, col_first, cols_here, 0)[None, :]
    row_chain = lax.dynamic_slice_in_dim(chain_ids, row_first, rows_here, 0)
    col_chain = lax.dynamic_slice_in_dim(chain_ids, col_first, cols_here, 0)[:, None]
    chain_term = chain_term[None, :]
    proj_t = proj.transpose(0, 2, 1)
    hid_gain = hid_gain[:, :, None]
    hid_bias = hid_bias[:, :, None]

    tile = 16
    smem = pl.BlockSpec(memory_space=pltpu.SMEM)
    whole = pl.BlockSpec(memory_space=pltpu.VMEM)
    pixels = pl.BlockSpec((tile, cols_here, width), lambda i: (i, 0, 0))
    planes = pl.BlockSpec((hidden, tile, cols_here), lambda i: (0, i, 0))
    planes_shape = jax.ShapeDtypeStruct((hidden, rows_here, cols_here), jnp.bfloat16)
    pixels_shape = jax.ShapeDtypeStruct(pair.shape, jnp.float32)
    rows_scratch = pltpu.VMEM((tile, hidden, cols_here), jnp.bfloat16)
    grid = (rows_here // tile,)
    params = pltpu.CompilerParams(vmem_limit_bytes=VMEM_LIMIT)

    left, right = pl.pallas_call(
        first_kernel,
        grid=grid,
        in_specs=[smem, smem, pixels] + [whole] * 6,
        out_specs=[planes, planes],
        out_shape=[planes_shape, planes_shape],
        scratch_shapes=[rows_scratch] * 2,
        compiler_params=params,
        name="first_projection",
    )(row_chain, row_real, pair, col_chain, col_real, chain_term, in_gain, in_bias, proj_t[0])
    mixed = triangle(left, right, True)
    state, left, right = pl.pallas_call(
        middle_kernel,
        grid=grid,
        in_specs=[smem, smem, pixels, planes] + [whole] * 10,
        out_specs=[pixels, planes, planes],
        out_shape=[pixels_shape, planes_shape, planes_shape],
        scratch_shapes=[rows_scratch] * 3,
        compiler_params=params,
        name="update_and_projection",
    )(
        row_chain, row_real, pair, mixed, col_chain, col_real, chain_term, in_gain, in_bias,
        proj_t[1], gate_w[0], hid_gain[0], hid_bias[0], out_w[0],
    )
    mixed = triangle(left, right, False)
    return pl.pallas_call(
        last_kernel,
        grid=grid,
        in_specs=[pixels, planes] + [whole] * 6,
        out_specs=pixels,
        out_shape=pixels_shape,
        scratch_shapes=[rows_scratch],
        compiler_params=params,
        name="last_update",
    )(state, mixed, in_gain, in_bias, gate_w[1], hid_gain[1], hid_bias[1], out_w[1])


def solution(mesh):
    return jax.shard_map(
        body,
        mesh=mesh,
        in_specs=(P(("grp", "row"), "col", None), P("grp"), P("grp")) + (P(),) * 8,
        out_specs=P(("grp", "row"), "col", None),
        check_vma=False,
    )
```

```python
import functools

import jax
import jax.numpy as jnp
from jax import lax
from jax.experimental import pallas as pl
from jax.experimental.pallas import tpu as pltpu
from jax.sharding import PartitionSpec as P

EPSILON = 1e-05
VMEM_LIMIT = 56 * 1024 * 1024


def norm(values, gain, bias, axis):
    center = values - jnp.mean(values, axis=axis, keepdims=True)
    variance = jnp.mean(center * center, axis=axis, keepdims=True)
    return center * lax.rsqrt(variance + EPSILON) * gain + bias


def dot(a, b, dims):
    return lax.dot_general(a, b, (dims, ((), ())), preferred_element_type=jnp.float32)


def project_row(row, normed, row_real, col_real, proj_t, left_rows, right_rows):
    hidden = left_rows.shape[1]
    mask = row_real * col_real
    both = dot(proj_t[...], normed, ((1,), (1,)))
    left = mask * jax.nn.sigmoid(both[:hidden]) * both[hidden : 2 * hidden]
    right = mask * jax.nn.sigmoid(both[2 * hidden : 3 * hidden]) * both[3 * hidden :]
    left_rows[row] = left.astype(jnp.bfloat16)
    right_rows[row] = right.astype(jnp.bfloat16)


def add_chain(pair_row, row_chain, col_chain, chain_term):
    same = (col_chain[...] == row_chain).astype(jnp.float32)
    return pair_row + same * chain_term[...]


def update_row(state, mixed, gain, bias, gate_w, hid_gain, hid_bias, out_w):
    normed = norm(state, gain, bias, -1).astype(jnp.bfloat16)
    gate = jax.nn.sigmoid(dot(normed, gate_w, ((1,), (0,))))
    normed_mix = norm(mixed.astype(jnp.float32), hid_gain, hid_bias, 0).astype(jnp.bfloat16)
    return state + gate * dot(normed_mix, out_w, ((0,), (0,)))


def first_kernel(
    chain_s, real_s, pair, col_chain, col_real, chain_term, gain, bias, proj_t,
    left, right, left_rows, right_rows,
):
    rows = pair.shape[0]
    base = pl.program_id(0) * rows

    @pl.loop(0, rows)
    def _(row):
        state = add_chain(pair[row], chain_s[base + row], col_chain, chain_term)
        normed = norm(state, gain[0:1], bias[0:1], -1).astype(jnp.bfloat16)
        project_row(row, normed, real_s[base + row], col_real[...], proj_t, left_rows, right_rows)

    left[...] = jnp.swapaxes(left_rows[...], 0, 1)
    right[...] = jnp.swapaxes(right_rows[...], 0, 1)


def middle_kernel(
    chain_s, real_s, pair, mixed, col_chain, col_real, chain_term, gain, bias, proj_t,
    gate_w, hid_gain, hid_bias, out_w,
    state_out, left, right, left_rows, right_rows, mixed_rows,
):
    rows = pair.shape[0]
    base = pl.program_id(0) * rows
    mixed_rows[...] = jnp.swapaxes(mixed[...], 0, 1)

    @pl.loop(0, rows)
    def _(row):
        state = add_chain(pair[row], chain_s[base + row], col_chain, chain_term)
        state = update_row(
            state, mixed_rows[row], gain[0:1], bias[0:1], gate_w[...], hid_gain[...],
            hid_bias[...], out_w[...],
        )
        state_out[row] = state
        normed = norm(state, gain[1:2], bias[1:2], -1).astype(jnp.bfloat16)
        project_row(row, normed, real_s[base + row], col_real[...], proj_t, left_rows, right_rows)

    left[...] = jnp.swapaxes(left_rows[...], 0, 1)
    right[...] = jnp.swapaxes(right_rows[...], 0, 1)


def last_kernel(
    state_in, mixed, gain, bias, gate_w, hid_gain, hid_bias, out_w, state_out, mixed_rows
):
    rows = state_in.shape[0]
    mixed_rows[...] = jnp.swapaxes(mixed[...], 0, 1)

    @pl.loop(0, rows)
    def _(row):
        state_out[row] = update_row(
            state_in[row], mixed_rows[row], gain[1:2], bias[1:2], gate_w[...], hid_gain[...],
            hid_bias[...], out_w[...],
        )


def triangle_kernel(
    outgoing, groups, parts, left, right, mixed,
    left_all, right_all, away, landed, result,
    send_sem, side_sem, away_send, away_recv, back_send, back_recv,
):
    cols, per_device, half, cols_here = left_all.shape
    rows_here = left.shape[1]
    grp, row, col = lax.axis_index("grp"), lax.axis_index("row"), lax.axis_index("col")
    inner = lax.axis_size("row") // 4
    plane = row // inner
    place = lax.rem(row, inner) * cols + col
    is_middle = (plane == 1) | (plane == 2)
    upper = plane // 2
    middle = 1 + upper
    chunk = per_device // parts

    def device(to_plane, to_place):
        return (grp, to_plane * inner + to_place // cols, lax.rem(to_place, cols))

    def row_offset(at_plane, at_row):
        return pl.multiple_of((lax.rem(at_plane, 2) * inner + at_row) * rows_here, rows_here)

    me = row * cols + col
    total = 4 * groups
    barrier = pltpu.get_barrier_semaphore()

    @pl.loop(1, total)
    def _(step):
        to = lax.rem(me + step, total)
        pl.semaphore_signal(
            barrier, inc=1, device_id=(grp, to // cols, lax.rem(to, cols)),
            device_id_type=pl.DeviceIdType.MESH,
        )

    pl.semaphore_wait(barrier, total - 1)

    my_offset = row_offset(plane, lax.rem(row, inner))

    @pl.loop(0, parts)
    def _(part):
        order = ((right, right_all, 1), (left, left_all, 0))
        for source, target, side in order:
            for step in range(groups):
                to = lax.rem(place + step, groups)
                src = source.at[pl.ds(to * per_device + part * chunk, chunk)]
                dst = target.at[col, pl.ds(part * chunk, chunk), pl.ds(my_offset, rows_here)]

                def send(src=src, dst=dst, to=to, side=side):
                    pltpu.make_async_remote_copy(
                        src_ref=src, dst_ref=dst, send_sem=send_sem.at[side, part],
                        recv_sem=side_sem.at[side, part], device_id=device(middle, to),
                        device_id_type=pl.DeviceIdType.MESH,
                    ).start()

                def keep(src=src, dst=dst, side=side):
                    pltpu.make_async_copy(src, dst, side_sem.at[side, part]).start()

                if step == 0:
                    pl.when(is_middle)(keep)
                    pl.when(jnp.logical_not(is_middle))(send)
                else:
                    send()

    def landed_side(ref, side, part):
        span = ref.at[:, pl.ds(part * chunk, chunk)]
        pltpu.make_async_copy(span, span, side_sem.at[side, part]).wait()

    leaving = right_all if outgoing else away

    def across(part):
        span = pl.ds(part * chunk, chunk)
        return pltpu.make_async_remote_copy(
            src_ref=leaving.at[:, span], dst_ref=landed.at[:, span],
            send_sem=away_send.at[part], recv_sem=away_recv.at[part],
            device_id=device(3 - middle, place), device_id_type=pl.DeviceIdType.MESH,
        )

    def begin(part):
        landed_side(right_all, 1, part)
        if not outgoing:
            landed_side(left_all, 0, part)

            @pl.loop(0, chunk)
            def _(index):
                channel = part * chunk + index
                ours = left_all[1 - upper, channel]
                for c in range(cols):
                    away[c, channel] = dot(
                        ours, right_all[c, channel], ((0,), (0,))
                    ).astype(jnp.bfloat16)

        across(part).start()

    def finish(part):
        if outgoing:
            landed_side(left_all, 0, part)
        across(part).wait_recv()

        @pl.loop(0, chunk)
        def _(index):
            channel = part * chunk + index
            if outgoing:
                for held, half_index in ((right_all, upper), (landed, 1 - upper)):
                    value = dot(left_all[0, channel], held[0, channel], ((1,), (1,)))
                    for c in range(1, cols):
                        value += dot(left_all[c, channel], held[c, channel], ((1,), (1,)))
                    result[half_index, channel] = value.astype(jnp.bfloat16)
            else:
                ours = left_all[upper, channel]
                for c in range(cols):
                    value = dot(ours, right_all[c, channel], ((0,), (0,)))
                    value += landed[c, channel].astype(jnp.float32)
                    result[c, channel] = value.astype(jnp.bfloat16)

        for edge in (True, False):
            to_plane = 3 * upper if edge else middle
            for step in range(groups):
                to = lax.rem(place + step, groups)
                offset = row_offset(to_plane, to // cols)
                src = result.at[
                    lax.rem(to, cols), pl.ds(part * chunk, chunk), pl.ds(offset, rows_here)
                ]
                dst = mixed.at[pl.ds(place * per_device + part * chunk, chunk)]
                if step == 0 and not edge:
                    pltpu.make_async_copy(src, dst, back_recv).start()
                else:
                    pltpu.make_async_remote_copy(
                        src_ref=src, dst_ref=dst, send_sem=back_send.at[part],
                        recv_sem=back_recv, device_id=device(to_plane, to),
                        device_id_type=pl.DeviceIdType.MESH,
                    ).start()

    @pl.when(is_middle)
    def _():
        begin(0)

        @pl.loop(1, parts)
        def _(part):
            begin(part)
            finish(part - 1)

        finish(parts - 1)

        @pl.loop(0, parts)
        def _(part):
            across(part).wait_send()
            sent = mixed.at[pl.ds(0, (2 * groups - 1) * chunk)]
            pltpu.make_async_copy(sent, sent, back_send.at[part]).wait()

    @pl.loop(0, parts)
    def _(part):
        for side in range(2):
            for condition, count in ((is_middle, groups - 1), (jnp.logical_not(is_middle), groups)):
                @pl.when(condition)
                def _(count=count, side=side):
                    sent = left.at[pl.ds(0, count * chunk)]
                    pltpu.make_async_copy(sent, sent, send_sem.at[side, part]).wait()

    pltpu.make_async_copy(mixed, mixed, back_recv).wait()


def triangle(left, right, outgoing):
    hidden, rows_here, cols_here = left.shape
    row_count = lax.axis_size("row")
    col_count = lax.axis_size("col")
    groups = row_count // 4 * col_count
    per_device = hidden // groups
    parts = min(8, per_device)
    half = row_count // 2 * rows_here
    held = pltpu.VMEM((col_count, per_device, half, cols_here), jnp.bfloat16)
    small = pltpu.VMEM((16, 128), jnp.bfloat16)
    anywhere = pl.BlockSpec(memory_space=pl.ANY)
    sems = pltpu.SemaphoreType.DMA
    return pl.pallas_call(
        functools.partial(triangle_kernel, outgoing, groups, parts),
        in_specs=[anywhere, anywhere],
        out_specs=anywhere,
        out_shape=jax.ShapeDtypeStruct(left.shape, jnp.bfloat16),
        scratch_shapes=[
            held, held, small if outgoing else held, held, held,
            sems((2, parts)), sems((2, parts)), sems((parts,)), sems((parts,)), sems((parts,)), sems,
        ],
        compiler_params=pltpu.CompilerParams(
            collective_id=1 if outgoing else 2, has_side_effects=True,
            vmem_limit_bytes=VMEM_LIMIT,
        ),
        name="outgoing_product" if outgoing else "incoming_product",
    )(left, right)


def body(
    pair, token_count, chain_ids, chain_term, in_gain, in_bias, proj, gate_w, hid_gain,
    hid_bias, out_w,
):
    rows_here, cols_here, width = pair.shape
    hidden = proj.shape[2] // 4
    row_first = lax.axis_index("row") * rows_here
    col_first = lax.axis_index("col") * cols_here
    positions = jnp.arange(chain_ids.shape[0], dtype=jnp.int32)
    real = (positions < token_count[0]).astype(jnp.float32)
    row_real = lax.dynamic_slice_in_dim(real, row_first, rows_here, 0)
    col_real = lax.dynamic_slice_in_dim(real, col_first, cols_here, 0)[None, :]
    row_chain = lax.dynamic_slice_in_dim(chain_ids, row_first, rows_here, 0)
    col_chain = lax.dynamic_slice_in_dim(chain_ids, col_first, cols_here, 0)[:, None]
    chain_term = chain_term[None, :]
    proj_t = proj.transpose(0, 2, 1)
    hid_gain = hid_gain[:, :, None]
    hid_bias = hid_bias[:, :, None]

    tile = 16
    smem = pl.BlockSpec(memory_space=pltpu.SMEM)
    whole = pl.BlockSpec(memory_space=pltpu.VMEM)
    pixels = pl.BlockSpec((tile, cols_here, width), lambda i: (i, 0, 0))
    planes = pl.BlockSpec((hidden, tile, cols_here), lambda i: (0, i, 0))
    planes_shape = jax.ShapeDtypeStruct((hidden, rows_here, cols_here), jnp.bfloat16)
    pixels_shape = jax.ShapeDtypeStruct(pair.shape, jnp.float32)
    rows_scratch = pltpu.VMEM((tile, hidden, cols_here), jnp.bfloat16)
    grid = (rows_here // tile,)
    params = pltpu.CompilerParams(vmem_limit_bytes=VMEM_LIMIT)

    left, right = pl.pallas_call(
        first_kernel,
        grid=grid,
        in_specs=[smem, smem, pixels] + [whole] * 6,
        out_specs=[planes, planes],
        out_shape=[planes_shape, planes_shape],
        scratch_shapes=[rows_scratch] * 2,
        compiler_params=params,
        name="first_projection",
    )(row_chain, row_real, pair, col_chain, col_real, chain_term, in_gain, in_bias, proj_t[0])
    mixed = triangle(left, right, True)
    state, left, right = pl.pallas_call(
        middle_kernel,
        grid=grid,
        in_specs=[smem, smem, pixels, planes] + [whole] * 10,
        out_specs=[pixels, planes, planes],
        out_shape=[pixels_shape, planes_shape, planes_shape],
        scratch_shapes=[rows_scratch] * 3,
        compiler_params=params,
        name="update_and_projection",
    )(
        row_chain, row_real, pair, mixed, col_chain, col_real, chain_term, in_gain, in_bias,
        proj_t[1], gate_w[0], hid_gain[0], hid_bias[0], out_w[0],
    )
    mixed = triangle(left, right, False)
    return pl.pallas_call(
        last_kernel,
        grid=grid,
        in_specs=[pixels, planes] + [whole] * 6,
        out_specs=pixels,
        out_shape=pixels_shape,
        scratch_shapes=[rows_scratch],
        compiler_params=params,
        name="last_update",
    )(state, mixed, in_gain, in_bias, gate_w[1], hid_gain[1], hid_bias[1], out_w[1])


def solution(mesh):
    return jax.shard_map(
        body,
        mesh=mesh,
        in_specs=(P(("grp", "row"), "col", None), P("grp"), P("grp")) + (P(),) * 8,
        out_specs=P(("grp", "row"), "col", None),
        check_vma=False,
    )
```

```python
import functools

import jax
import jax.numpy as jnp
from jax import lax
from jax.experimental import pallas as pl
from jax.experimental.pallas import tpu as pltpu
from jax.sharding import PartitionSpec as P

EPSILON = 1e-05
VMEM_LIMIT = 56 * 1024 * 1024


def norm(values, gain, bias, axis):
    center = values - jnp.mean(values, axis=axis, keepdims=True)
    variance = jnp.mean(center * center, axis=axis, keepdims=True)
    return center * lax.rsqrt(variance + EPSILON) * gain + bias


def sigmoid(values):
    return 0.5 + 0.5 * jnp.tanh(0.5 * values)


def dot(a, b, dims):
    return lax.dot_general(a, b, (dims, ((), ())), preferred_element_type=jnp.float32)


def project_row(row, normed, row_real, col_real, proj_t, left_rows, right_rows):
    hidden = left_rows.shape[1]
    mask = row_real * col_real
    both = dot(proj_t[...], normed, ((1,), (1,)))
    left = mask * sigmoid(both[:hidden]) * both[hidden : 2 * hidden]
    right = mask * sigmoid(both[2 * hidden : 3 * hidden]) * both[3 * hidden :]
    left_rows[row] = left.astype(jnp.bfloat16)
    right_rows[row] = right.astype(jnp.bfloat16)


def add_chain(pair_row, row_chain, col_chain, chain_term):
    same = (col_chain[...] == row_chain).astype(jnp.float32)
    return pair_row + same * chain_term[...]


def update_row(state, mixed, gain, bias, gate_w, hid_gain, hid_bias, out_w):
    normed = norm(state, gain, bias, -1).astype(jnp.bfloat16)
    gate = sigmoid(dot(normed, gate_w, ((1,), (0,))))
    normed_mix = norm(mixed.astype(jnp.float32), hid_gain, hid_bias, 0).astype(jnp.bfloat16)
    return state + gate * dot(normed_mix, out_w, ((0,), (0,)))


def first_kernel(
    chain_s, real_s, pair, col_chain, col_real, chain_term, gain, bias, proj_t,
    left, right, left_rows, right_rows,
):
    rows = pair.shape[0]
    base = pl.program_id(0) * rows

    @pl.loop(0, rows, unroll=4)
    def _(row):
        state = add_chain(pair[row], chain_s[base + row], col_chain, chain_term)
        normed = norm(state, gain[0:1], bias[0:1], -1).astype(jnp.bfloat16)
        project_row(row, normed, real_s[base + row], col_real[...], proj_t, left_rows, right_rows)

    left[...] = jnp.swapaxes(left_rows[...], 0, 1)
    right[...] = jnp.swapaxes(right_rows[...], 0, 1)


def middle_kernel(
    chain_s, real_s, pair, mixed, col_chain, col_real, chain_term, gain, bias, proj_t,
    gate_w, hid_gain, hid_bias, out_w,
    state_out, left, right, left_rows, right_rows, mixed_rows,
):
    rows = pair.shape[0]
    base = pl.program_id(0) * rows
    mixed_rows[...] = jnp.swapaxes(mixed[...], 0, 1)

    @pl.loop(0, rows, unroll=4)
    def _(row):
        state = add_chain(pair[row], chain_s[base + row], col_chain, chain_term)
        state = update_row(
            state, mixed_rows[row], gain[0:1], bias[0:1], gate_w[...], hid_gain[...],
            hid_bias[...], out_w[...],
        )
        state_out[row] = state
        normed = norm(state, gain[1:2], bias[1:2], -1).astype(jnp.bfloat16)
        project_row(row, normed, real_s[base + row], col_real[...], proj_t, left_rows, right_rows)

    left[...] = jnp.swapaxes(left_rows[...], 0, 1)
    right[...] = jnp.swapaxes(right_rows[...], 0, 1)


def last_kernel(
    state_in, mixed, gain, bias, gate_w, hid_gain, hid_bias, out_w, state_out, mixed_rows
):
    rows = state_in.shape[0]
    mixed_rows[...] = jnp.swapaxes(mixed[...], 0, 1)

    @pl.loop(0, rows, unroll=4)
    def _(row):
        state_out[row] = update_row(
            state_in[row], mixed_rows[row], gain[1:2], bias[1:2], gate_w[...], hid_gain[...],
            hid_bias[...], out_w[...],
        )


def triangle_kernel(
    outgoing, groups, parts, left, right, mixed,
    left_all, right_all, away, landed, result,
    send_sem, side_sem, away_send, away_recv, back_send, back_recv,
):
    cols, per_device, half, cols_here = left_all.shape
    rows_here = left.shape[1]
    grp, row, col = lax.axis_index("grp"), lax.axis_index("row"), lax.axis_index("col")
    inner = lax.axis_size("row") // 4
    plane = row // inner
    place = lax.rem(row, inner) * cols + col
    is_middle = (plane == 1) | (plane == 2)
    upper = plane // 2
    middle = 1 + upper
    chunk = per_device // parts

    def device(to_plane, to_place):
        return (grp, to_plane * inner + to_place // cols, lax.rem(to_place, cols))

    def row_offset(at_plane, at_row):
        return pl.multiple_of((lax.rem(at_plane, 2) * inner + at_row) * rows_here, rows_here)

    me = row * cols + col
    total = 4 * groups
    barrier = pltpu.get_barrier_semaphore()

    @pl.loop(1, total)
    def _(step):
        to = lax.rem(me + step, total)
        pl.semaphore_signal(
            barrier, inc=1, device_id=(grp, to // cols, lax.rem(to, cols)),
            device_id_type=pl.DeviceIdType.MESH,
        )

    pl.semaphore_wait(barrier, total - 1)

    my_offset = row_offset(plane, lax.rem(row, inner))

    @pl.loop(0, parts)
    def _(part):
        order = ((right, right_all, 1), (left, left_all, 0))
        for source, target, side in order:
            for step in range(groups):
                to = lax.rem(place + step, groups)
                src = source.at[pl.ds(to * per_device + part * chunk, chunk)]
                dst = target.at[col, pl.ds(part * chunk, chunk), pl.ds(my_offset, rows_here)]

                def send(src=src, dst=dst, to=to, side=side):
                    pltpu.make_async_remote_copy(
                        src_ref=src, dst_ref=dst, send_sem=send_sem.at[side, part],
                        recv_sem=side_sem.at[side, part], device_id=device(middle, to),
                        device_id_type=pl.DeviceIdType.MESH,
                    ).start()

                def keep(src=src, dst=dst, side=side):
                    pltpu.make_async_copy(src, dst, side_sem.at[side, part]).start()

                if step == 0:
                    pl.when(is_middle)(keep)
                    pl.when(jnp.logical_not(is_middle))(send)
                else:
                    send()

    def landed_side(ref, side, part):
        span = ref.at[:, pl.ds(part * chunk, chunk)]
        pltpu.make_async_copy(span, span, side_sem.at[side, part]).wait()

    leaving = right_all if outgoing else away

    def across(part):
        span = pl.ds(part * chunk, chunk)
        return pltpu.make_async_remote_copy(
            src_ref=leaving.at[:, span], dst_ref=landed.at[:, span],
            send_sem=away_send.at[part], recv_sem=away_recv.at[part],
            device_id=device(3 - middle, place), device_id_type=pl.DeviceIdType.MESH,
        )

    def begin(part):
        landed_side(right_all, 1, part)
        if not outgoing:
            landed_side(left_all, 0, part)

            @pl.loop(0, chunk)
            def _(index):
                channel = part * chunk + index
                ours = left_all[1 - upper, channel]
                for c in range(cols):
                    away[c, channel] = dot(
                        ours, right_all[c, channel], ((0,), (0,))
                    ).astype(jnp.bfloat16)

        across(part).start()

    def finish(part):
        if outgoing:
            landed_side(left_all, 0, part)
        across(part).wait_recv()

        @pl.loop(0, chunk)
        def _(index):
            channel = part * chunk + index
            if outgoing:
                for held, half_index in ((right_all, upper), (landed, 1 - upper)):
                    value = dot(left_all[0, channel], held[0, channel], ((1,), (1,)))
                    for c in range(1, cols):
                        value += dot(left_all[c, channel], held[c, channel], ((1,), (1,)))
                    result[half_index, channel] = value.astype(jnp.bfloat16)
            else:
                ours = left_all[upper, channel]
                for c in range(cols):
                    value = dot(ours, right_all[c, channel], ((0,), (0,)))
                    value += landed[c, channel].astype(jnp.float32)
                    result[c, channel] = value.astype(jnp.bfloat16)

        for edge in (True, False):
            to_plane = 3 * upper if edge else middle
            for step in range(groups):
                to = lax.rem(place + step, groups)
                offset = row_offset(to_plane, to // cols)
                src = result.at[
                    lax.rem(to, cols), pl.ds(part * chunk, chunk), pl.ds(offset, rows_here)
                ]
                dst = mixed.at[pl.ds(place * per_device + part * chunk, chunk)]
                if step == 0 and not edge:
                    pltpu.make_async_copy(src, dst, back_recv).start()
                else:
                    pltpu.make_async_remote_copy(
                        src_ref=src, dst_ref=dst, send_sem=back_send.at[part],
                        recv_sem=back_recv, device_id=device(to_plane, to),
                        device_id_type=pl.DeviceIdType.MESH,
                    ).start()

    @pl.when(is_middle)
    def _():
        begin(0)

        @pl.loop(1, parts)
        def _(part):
            begin(part)
            finish(part - 1)

        finish(parts - 1)

        @pl.loop(0, parts)
        def _(part):
            across(part).wait_send()
            sent = mixed.at[pl.ds(0, (2 * groups - 1) * chunk)]
            pltpu.make_async_copy(sent, sent, back_send.at[part]).wait()

    @pl.loop(0, parts)
    def _(part):
        for side in range(2):
            for condition, count in ((is_middle, groups - 1), (jnp.logical_not(is_middle), groups)):
                @pl.when(condition)
                def _(count=count, side=side):
                    sent = left.at[pl.ds(0, count * chunk)]
                    pltpu.make_async_copy(sent, sent, send_sem.at[side, part]).wait()

    pltpu.make_async_copy(mixed, mixed, back_recv).wait()


def triangle(left, right, outgoing):
    hidden, rows_here, cols_here = left.shape
    row_count = lax.axis_size("row")
    col_count = lax.axis_size("col")
    groups = row_count // 4 * col_count
    per_device = hidden // groups
    parts = min(16, per_device)
    half = row_count // 2 * rows_here
    held = pltpu.VMEM((col_count, per_device, half, cols_here), jnp.bfloat16)
    small = pltpu.VMEM((16, 128), jnp.bfloat16)
    anywhere = pl.BlockSpec(memory_space=pl.ANY)
    sems = pltpu.SemaphoreType.DMA
    return pl.pallas_call(
        functools.partial(triangle_kernel, outgoing, groups, parts),
        in_specs=[anywhere, anywhere],
        out_specs=anywhere,
        out_shape=jax.ShapeDtypeStruct(left.shape, jnp.bfloat16),
        scratch_shapes=[
            held, held, small if outgoing else held, held, held,
            sems((2, parts)), sems((2, parts)), sems((parts,)), sems((parts,)), sems((parts,)), sems,
        ],
        compiler_params=pltpu.CompilerParams(
            collective_id=1 if outgoing else 2, has_side_effects=True,
            vmem_limit_bytes=VMEM_LIMIT,
        ),
        name="outgoing_product" if outgoing else "incoming_product",
    )(left, right)


def body(
    pair, token_count, chain_ids, chain_term, in_gain, in_bias, proj, gate_w, hid_gain,
    hid_bias, out_w,
):
    rows_here, cols_here, width = pair.shape
    hidden = proj.shape[2] // 4
    row_first = lax.axis_index("row") * rows_here
    col_first = lax.axis_index("col") * cols_here
    positions = jnp.arange(chain_ids.shape[0], dtype=jnp.int32)
    real = (positions < token_count[0]).astype(jnp.float32)
    row_real = lax.dynamic_slice_in_dim(real, row_first, rows_here, 0)
    col_real = lax.dynamic_slice_in_dim(real, col_first, cols_here, 0)[None, :]
    row_chain = lax.dynamic_slice_in_dim(chain_ids, row_first, rows_here, 0)
    col_chain = lax.dynamic_slice_in_dim(chain_ids, col_first, cols_here, 0)[:, None]
    chain_term = chain_term[None, :]
    proj_t = proj.transpose(0, 2, 1)
    hid_gain = hid_gain[:, :, None]
    hid_bias = hid_bias[:, :, None]

    tile = 16
    smem = pl.BlockSpec(memory_space=pltpu.SMEM)
    whole = pl.BlockSpec(memory_space=pltpu.VMEM)
    pixels = pl.BlockSpec((tile, cols_here, width), lambda i: (i, 0, 0))
    planes = pl.BlockSpec((hidden, tile, cols_here), lambda i: (0, i, 0))
    planes_shape = jax.ShapeDtypeStruct((hidden, rows_here, cols_here), jnp.bfloat16)
    pixels_shape = jax.ShapeDtypeStruct(pair.shape, jnp.float32)
    rows_scratch = pltpu.VMEM((tile, hidden, cols_here), jnp.bfloat16)
    grid = (rows_here // tile,)
    params = pltpu.CompilerParams(vmem_limit_bytes=VMEM_LIMIT)

    left, right = pl.pallas_call(
        first_kernel,
        grid=grid,
        in_specs=[smem, smem, pixels] + [whole] * 6,
        out_specs=[planes, planes],
        out_shape=[planes_shape, planes_shape],
        scratch_shapes=[rows_scratch] * 2,
        compiler_params=params,
        name="first_projection",
    )(row_chain, row_real, pair, col_chain, col_real, chain_term, in_gain, in_bias, proj_t[0])
    mixed = triangle(left, right, True)
    state, left, right = pl.pallas_call(
        middle_kernel,
        grid=grid,
        in_specs=[smem, smem, pixels, planes] + [whole] * 10,
        out_specs=[pixels, planes, planes],
        out_shape=[pixels_shape, planes_shape, planes_shape],
        scratch_shapes=[rows_scratch] * 3,
        compiler_params=params,
        name="update_and_projection",
    )(
        row_chain, row_real, pair, mixed, col_chain, col_real, chain_term, in_gain, in_bias,
        proj_t[1], gate_w[0], hid_gain[0], hid_bias[0], out_w[0],
    )
    mixed = triangle(left, right, False)
    return pl.pallas_call(
        last_kernel,
        grid=grid,
        in_specs=[pixels, planes] + [whole] * 6,
        out_specs=pixels,
        out_shape=pixels_shape,
        scratch_shapes=[rows_scratch],
        compiler_params=params,
        name="last_update",
    )(state, mixed, in_gain, in_bias, gate_w[1], hid_gain[1], hid_bias[1], out_w[1])


def solution(mesh):
    return jax.shard_map(
        body,
        mesh=mesh,
        in_specs=(P(("grp", "row"), "col", None), P("grp"), P("grp")) + (P(),) * 8,
        out_specs=P(("grp", "row"), "col", None),
        check_vma=False,
    )
```

```python
import functools

import jax
import jax.numpy as jnp
from jax import lax
from jax.experimental import pallas as pl
from jax.experimental.pallas import tpu as pltpu
from jax.sharding import PartitionSpec as P

EPSILON = 1e-05
VMEM_LIMIT = 56 * 1024 * 1024


def norm(values, gain, bias, axis):
    center = values - jnp.mean(values, axis=axis, keepdims=True)
    variance = jnp.mean(center * center, axis=axis, keepdims=True)
    return center * lax.rsqrt(variance + EPSILON) * gain + bias


def sigmoid(values):
    return 0.5 + 0.5 * jnp.tanh(0.5 * values)


def dot(a, b, dims):
    return lax.dot_general(a, b, (dims, ((), ())), preferred_element_type=jnp.float32)


def project_row(row, normed, row_real, col_real, proj_t, left_rows, right_rows):
    hidden = left_rows.shape[1]
    mask = row_real * col_real
    both = dot(proj_t[...], normed, ((1,), (1,)))
    left = mask * sigmoid(both[:hidden]) * both[hidden : 2 * hidden]
    right = mask * sigmoid(both[2 * hidden : 3 * hidden]) * both[3 * hidden :]
    left_rows[row] = left.astype(jnp.bfloat16)
    right_rows[row] = right.astype(jnp.bfloat16)


def add_chain(pair_row, row_chain, col_chain, chain_term):
    same = (col_chain[...] == row_chain).astype(jnp.float32)
    return pair_row + same * chain_term[...]


def update_row(state, mixed, gain, bias, gate_w, hid_gain, hid_bias, out_w):
    normed = norm(state, gain, bias, -1).astype(jnp.bfloat16)
    gate = sigmoid(dot(normed, gate_w, ((1,), (0,))))
    normed_mix = norm(mixed.astype(jnp.float32), hid_gain, hid_bias, 0).astype(jnp.bfloat16)
    return state + gate * dot(normed_mix, out_w, ((0,), (0,)))


def first_kernel(
    chain_s, real_s, pair, col_chain, col_real, chain_term, gain, bias, proj_t,
    left, right, left_rows, right_rows,
):
    rows = pair.shape[0]
    base = pl.program_id(0) * rows

    @pl.loop(0, rows, unroll=8)
    def _(row):
        state = add_chain(pair[row], chain_s[base + row], col_chain, chain_term)
        normed = norm(state, gain[0:1], bias[0:1], -1).astype(jnp.bfloat16)
        project_row(row, normed, real_s[base + row], col_real[...], proj_t, left_rows, right_rows)

    left[...] = jnp.swapaxes(left_rows[...], 0, 1)
    right[...] = jnp.swapaxes(right_rows[...], 0, 1)


def middle_kernel(
    chain_s, real_s, pair, mixed, col_chain, col_real, chain_term, gain, bias, proj_t,
    gate_w, hid_gain, hid_bias, out_w,
    state_out, left, right, left_rows, right_rows, mixed_rows,
):
    rows = pair.shape[0]
    base = pl.program_id(0) * rows
    mixed_rows[...] = jnp.swapaxes(mixed[...], 0, 1)

    @pl.loop(0, rows, unroll=8)
    def _(row):
        state = add_chain(pair[row], chain_s[base + row], col_chain, chain_term)
        state = update_row(
            state, mixed_rows[row], gain[0:1], bias[0:1], gate_w[...], hid_gain[...],
            hid_bias[...], out_w[...],
        )
        state_out[row] = state
        normed = norm(state, gain[1:2], bias[1:2], -1).astype(jnp.bfloat16)
        project_row(row, normed, real_s[base + row], col_real[...], proj_t, left_rows, right_rows)

    left[...] = jnp.swapaxes(left_rows[...], 0, 1)
    right[...] = jnp.swapaxes(right_rows[...], 0, 1)


def last_kernel(
    state_in, mixed, gain, bias, gate_w, hid_gain, hid_bias, out_w, state_out, mixed_rows
):
    rows = state_in.shape[0]
    mixed_rows[...] = jnp.swapaxes(mixed[...], 0, 1)

    @pl.loop(0, rows, unroll=8)
    def _(row):
        state_out[row] = update_row(
            state_in[row], mixed_rows[row], gain[1:2], bias[1:2], gate_w[...], hid_gain[...],
            hid_bias[...], out_w[...],
        )


def triangle_kernel(
    outgoing, groups, parts, left, right, mixed,
    left_all, right_all, away, landed, result,
    send_sem, side_sem, edge_send, away_send, away_recv, back_send, back_recv,
):
    cols, per_device, half, cols_here = left_all.shape
    rows_here = left.shape[1]
    grp, row, col = lax.axis_index("grp"), lax.axis_index("row"), lax.axis_index("col")
    inner = lax.axis_size("row") // 4
    plane = row // inner
    place = lax.rem(row, inner) * cols + col
    is_middle = (plane == 1) | (plane == 2)
    upper = plane // 2
    middle = 1 + upper
    chunk = per_device // parts

    def device(to_plane, to_place):
        return (grp, to_plane * inner + to_place // cols, lax.rem(to_place, cols))

    def row_offset(at_plane, at_row):
        return pl.multiple_of((lax.rem(at_plane, 2) * inner + at_row) * rows_here, rows_here)

    me = row * cols + col
    total = 4 * groups
    barrier = pltpu.get_barrier_semaphore()

    @pl.loop(1, total)
    def _(step):
        to = lax.rem(me + step, total)
        pl.semaphore_signal(
            barrier, inc=1, device_id=(grp, to // cols, lax.rem(to, cols)),
            device_id_type=pl.DeviceIdType.MESH,
        )

    pl.semaphore_wait(barrier, total - 1)

    my_offset = row_offset(plane, lax.rem(row, inner))

    @pl.loop(0, parts)
    def _(part):
        order = ((right, right_all, 1), (left, left_all, 0))
        for source, target, side in order:
            for step in range(groups):
                to = lax.rem(place + step, groups)
                src = source.at[pl.ds(to * per_device + part * chunk, chunk)]
                dst = target.at[col, pl.ds(part * chunk, chunk), pl.ds(my_offset, rows_here)]

                def send(src=src, dst=dst, to=to, side=side):
                    pltpu.make_async_remote_copy(
                        src_ref=src, dst_ref=dst, send_sem=send_sem.at[side, part],
                        recv_sem=side_sem.at[side, part], device_id=device(plane, to),
                        device_id_type=pl.DeviceIdType.MESH,
                    ).start()

                def keep(src=src, dst=dst, side=side):
                    pltpu.make_async_copy(src, dst, side_sem.at[side, part]).start()

                if step == 0:
                    keep()
                else:
                    send()

    def landed_side(ref, side, part):
        span = ref.at[:, pl.ds(part * chunk, chunk)]
        pltpu.make_async_copy(span, span, side_sem.at[side, part]).wait()

    plane_rows = pl.ds(
        pl.multiple_of(lax.rem(plane, 2) * inner * rows_here, rows_here), inner * rows_here
    )

    def forward(ref, side, part):
        span = ref.at[:, pl.ds(part * chunk, chunk), plane_rows]
        return pltpu.make_async_remote_copy(
            src_ref=span, dst_ref=span, send_sem=edge_send.at[side, part],
            recv_sem=side_sem.at[side, part], device_id=device(middle, place),
            device_id_type=pl.DeviceIdType.MESH,
        )

    @pl.when(jnp.logical_not(is_middle))
    def _():
        @pl.loop(0, parts)
        def _(part):
            for ref, side in ((right_all, 1), (left_all, 0)):
                span = ref.at[:, pl.ds(part * chunk, chunk), plane_rows]
                pltpu.make_async_copy(span, span, side_sem.at[side, part]).wait()
                forward(ref, side, part).start()

    leaving = right_all if outgoing else away

    def across(part):
        span = pl.ds(part * chunk, chunk)
        return pltpu.make_async_remote_copy(
            src_ref=leaving.at[:, span], dst_ref=landed.at[:, span],
            send_sem=away_send.at[part], recv_sem=away_recv.at[part],
            device_id=device(3 - middle, place), device_id_type=pl.DeviceIdType.MESH,
        )

    def begin(part):
        landed_side(right_all, 1, part)
        if not outgoing:
            landed_side(left_all, 0, part)

            @pl.loop(0, chunk)
            def _(index):
                channel = part * chunk + index
                ours = left_all[1 - upper, channel]
                for c in range(cols):
                    away[c, channel] = dot(
                        ours, right_all[c, channel], ((0,), (0,))
                    ).astype(jnp.bfloat16)

        across(part).start()

    def finish(part):
        if outgoing:
            landed_side(left_all, 0, part)
        across(part).wait_recv()

        @pl.loop(0, chunk)
        def _(index):
            channel = part * chunk + index
            if outgoing:
                for held, half_index in ((right_all, upper), (landed, 1 - upper)):
                    value = dot(left_all[0, channel], held[0, channel], ((1,), (1,)))
                    for c in range(1, cols):
                        value += dot(left_all[c, channel], held[c, channel], ((1,), (1,)))
                    result[half_index, channel] = value.astype(jnp.bfloat16)
            else:
                ours = left_all[upper, channel]
                for c in range(cols):
                    value = dot(ours, right_all[c, channel], ((0,), (0,)))
                    value += landed[c, channel].astype(jnp.float32)
                    result[c, channel] = value.astype(jnp.bfloat16)

        for edge in (True, False):
            to_plane = 3 * upper if edge else middle
            for step in range(groups):
                to = lax.rem(place + step, groups)
                offset = row_offset(to_plane, to // cols)
                src = result.at[
                    lax.rem(to, cols), pl.ds(part * chunk, chunk), pl.ds(offset, rows_here)
                ]
                dst = mixed.at[pl.ds(place * per_device + part * chunk, chunk)]
                if step == 0 and not edge:
                    pltpu.make_async_copy(src, dst, back_recv).start()
                else:
                    pltpu.make_async_remote_copy(
                        src_ref=src, dst_ref=dst, send_sem=back_send.at[part],
                        recv_sem=back_recv, device_id=device(to_plane, to),
                        device_id_type=pl.DeviceIdType.MESH,
                    ).start()

    @pl.when(is_middle)
    def _():
        begin(0)

        @pl.loop(1, parts)
        def _(part):
            begin(part)
            finish(part - 1)

        finish(parts - 1)

        @pl.loop(0, parts)
        def _(part):
            across(part).wait_send()
            sent = mixed.at[pl.ds(0, (2 * groups - 1) * chunk)]
            pltpu.make_async_copy(sent, sent, back_send.at[part]).wait()

    @pl.loop(0, parts)
    def _(part):
        for side in range(2):
            sent = left.at[pl.ds(0, (groups - 1) * chunk)]
            pltpu.make_async_copy(sent, sent, send_sem.at[side, part]).wait()

    @pl.when(jnp.logical_not(is_middle))
    def _():
        @pl.loop(0, parts)
        def _(part):
            for ref, side in ((right_all, 1), (left_all, 0)):
                forward(ref, side, part).wait_send()

    pltpu.make_async_copy(mixed, mixed, back_recv).wait()


def triangle(left, right, outgoing):
    hidden, rows_here, cols_here = left.shape
    row_count = lax.axis_size("row")
    col_count = lax.axis_size("col")
    groups = row_count // 4 * col_count
    per_device = hidden // groups
    parts = min(16, per_device)
    half = row_count // 2 * rows_here
    held = pltpu.VMEM((col_count, per_device, half, cols_here), jnp.bfloat16)
    small = pltpu.VMEM((16, 128), jnp.bfloat16)
    anywhere = pl.BlockSpec(memory_space=pl.ANY)
    sems = pltpu.SemaphoreType.DMA
    return pl.pallas_call(
        functools.partial(triangle_kernel, outgoing, groups, parts),
        in_specs=[anywhere, anywhere],
        out_specs=anywhere,
        out_shape=jax.ShapeDtypeStruct(left.shape, jnp.bfloat16),
        scratch_shapes=[
            held, held, small if outgoing else held, held, held,
            sems((2, parts)), sems((2, parts)), sems((2, parts)), sems((parts,)), sems((parts,)), sems((parts,)), sems,
        ],
        compiler_params=pltpu.CompilerParams(
            collective_id=1 if outgoing else 2, has_side_effects=True,
            vmem_limit_bytes=VMEM_LIMIT,
        ),
        name="outgoing_product" if outgoing else "incoming_product",
    )(left, right)


def body(
    pair, token_count, chain_ids, chain_term, in_gain, in_bias, proj, gate_w, hid_gain,
    hid_bias, out_w,
):
    rows_here, cols_here, width = pair.shape
    hidden = proj.shape[2] // 4
    row_first = lax.axis_index("row") * rows_here
    col_first = lax.axis_index("col") * cols_here
    positions = jnp.arange(chain_ids.shape[0], dtype=jnp.int32)
    real = (positions < token_count[0]).astype(jnp.float32)
    row_real = lax.dynamic_slice_in_dim(real, row_first, rows_here, 0)
    col_real = lax.dynamic_slice_in_dim(real, col_first, cols_here, 0)[None, :]
    row_chain = lax.dynamic_slice_in_dim(chain_ids, row_first, rows_here, 0)
    col_chain = lax.dynamic_slice_in_dim(chain_ids, col_first, cols_here, 0)[:, None]
    chain_term = chain_term[None, :]
    proj_t = proj.transpose(0, 2, 1)
    hid_gain = hid_gain[:, :, None]
    hid_bias = hid_bias[:, :, None]

    tile = 16
    smem = pl.BlockSpec(memory_space=pltpu.SMEM)
    whole = pl.BlockSpec(memory_space=pltpu.VMEM)
    pixels = pl.BlockSpec((tile, cols_here, width), lambda i: (i, 0, 0))
    planes = pl.BlockSpec((hidden, tile, cols_here), lambda i: (0, i, 0))
    planes_shape = jax.ShapeDtypeStruct((hidden, rows_here, cols_here), jnp.bfloat16)
    pixels_shape = jax.ShapeDtypeStruct(pair.shape, jnp.float32)
    rows_scratch = pltpu.VMEM((tile, hidden, cols_here), jnp.bfloat16)
    grid = (rows_here // tile,)
    params = pltpu.CompilerParams(vmem_limit_bytes=VMEM_LIMIT)

    left, right = pl.pallas_call(
        first_kernel,
        grid=grid,
        in_specs=[smem, smem, pixels] + [whole] * 6,
        out_specs=[planes, planes],
        out_shape=[planes_shape, planes_shape],
        scratch_shapes=[rows_scratch] * 2,
        compiler_params=params,
        name="first_projection",
    )(row_chain, row_real, pair, col_chain, col_real, chain_term, in_gain, in_bias, proj_t[0])
    mixed = triangle(left, right, True)
    state, left, right = pl.pallas_call(
        middle_kernel,
        grid=grid,
        in_specs=[smem, smem, pixels, planes] + [whole] * 10,
        out_specs=[pixels, planes, planes],
        out_shape=[pixels_shape, planes_shape, planes_shape],
        scratch_shapes=[rows_scratch] * 3,
        compiler_params=params,
        name="update_and_projection",
    )(
        row_chain, row_real, pair, mixed, col_chain, col_real, chain_term, in_gain, in_bias,
        proj_t[1], gate_w[0], hid_gain[0], hid_bias[0], out_w[0],
    )
    mixed = triangle(left, right, False)
    return pl.pallas_call(
        last_kernel,
        grid=grid,
        in_specs=[pixels, planes] + [whole] * 6,
        out_specs=pixels,
        out_shape=pixels_shape,
        scratch_shapes=[rows_scratch],
        compiler_params=params,
        name="last_update",
    )(state, mixed, in_gain, in_bias, gate_w[1], hid_gain[1], hid_bias[1], out_w[1])


def solution(mesh):
    return jax.shard_map(
        body,
        mesh=mesh,
        in_specs=(P(("grp", "row"), "col", None), P("grp"), P("grp")) + (P(),) * 8,
        out_specs=P(("grp", "row"), "col", None),
        check_vma=False,
    )
```

```python
import functools

import jax
import jax.numpy as jnp
from jax import lax
from jax.experimental import pallas as pl
from jax.experimental.pallas import tpu as pltpu
from jax.sharding import PartitionSpec as P

EPSILON = 1e-05
VMEM_LIMIT = 56 * 1024 * 1024


def norm(values, gain, bias, axis):
    center = values - jnp.mean(values, axis=axis, keepdims=True)
    variance = jnp.mean(center * center, axis=axis, keepdims=True)
    return center * lax.rsqrt(variance + EPSILON) * gain + bias


def sigmoid(values):
    return 0.5 + 0.5 * jnp.tanh(0.5 * values)


def dot(a, b, dims):
    return lax.dot_general(a, b, (dims, ((), ())), preferred_element_type=jnp.float32)


def project_row(row, normed, row_real, col_real, proj_t, left_rows, right_rows):
    hidden = left_rows.shape[1]
    mask = row_real * col_real
    both = dot(proj_t[...], normed, ((1,), (1,)))
    left = mask * sigmoid(both[:hidden]) * both[hidden : 2 * hidden]
    right = mask * sigmoid(both[2 * hidden : 3 * hidden]) * both[3 * hidden :]
    left_rows[row] = left.astype(jnp.bfloat16)
    right_rows[row] = right.astype(jnp.bfloat16)


def add_chain(pair_row, row_chain, col_chain, chain_term):
    same = (col_chain[...] == row_chain).astype(jnp.float32)
    return pair_row + same * chain_term[...]


def update_row(state, mixed, gain, bias, gate_w, hid_gain, hid_bias, out_w):
    normed = norm(state, gain, bias, -1).astype(jnp.bfloat16)
    gate = sigmoid(dot(normed, gate_w, ((1,), (0,))))
    normed_mix = norm(mixed.astype(jnp.float32), hid_gain, hid_bias, 0).astype(jnp.bfloat16)
    return state + gate * dot(normed_mix, out_w, ((0,), (0,)))


def first_kernel(
    chain_s, real_s, pair, col_chain, col_real, chain_term, gain, bias, proj_t,
    left, right, left_rows, right_rows,
):
    rows = pair.shape[0]
    base = pl.program_id(0) * rows

    @pl.loop(0, rows, unroll=8)
    def _(row):
        state = add_chain(pair[row], chain_s[base + row], col_chain, chain_term)
        normed = norm(state, gain[0:1], bias[0:1], -1).astype(jnp.bfloat16)
        project_row(row, normed, real_s[base + row], col_real[...], proj_t, left_rows, right_rows)

    left[...] = jnp.swapaxes(left_rows[...], 0, 1)
    right[...] = jnp.swapaxes(right_rows[...], 0, 1)


def middle_kernel(
    chain_s, real_s, pair, mixed, col_chain, col_real, chain_term, gain, bias, proj_t,
    gate_w, hid_gain, hid_bias, out_w,
    state_out, left, right, left_rows, right_rows, mixed_rows,
):
    rows = pair.shape[0]
    base = pl.program_id(0) * rows
    mixed_rows[...] = jnp.swapaxes(mixed[...], 0, 1)

    @pl.loop(0, rows, unroll=8)
    def _(row):
        state = add_chain(pair[row], chain_s[base + row], col_chain, chain_term)
        state = update_row(
            state, mixed_rows[row], gain[0:1], bias[0:1], gate_w[...], hid_gain[...],
            hid_bias[...], out_w[...],
        )
        state_out[row] = state
        normed = norm(state, gain[1:2], bias[1:2], -1).astype(jnp.bfloat16)
        project_row(row, normed, real_s[base + row], col_real[...], proj_t, left_rows, right_rows)

    left[...] = jnp.swapaxes(left_rows[...], 0, 1)
    right[...] = jnp.swapaxes(right_rows[...], 0, 1)


def last_kernel(
    state_in, mixed, gain, bias, gate_w, hid_gain, hid_bias, out_w, state_out, mixed_rows
):
    rows = state_in.shape[0]
    mixed_rows[...] = jnp.swapaxes(mixed[...], 0, 1)

    @pl.loop(0, rows, unroll=8)
    def _(row):
        state_out[row] = update_row(
            state_in[row], mixed_rows[row], gain[1:2], bias[1:2], gate_w[...], hid_gain[...],
            hid_bias[...], out_w[...],
        )


def triangle_kernel(
    outgoing, groups, parts, left, right, mixed,
    left_all, right_all, away, landed, result,
    send_sem, side_sem, edge_send, away_send, away_recv, back_send, back_recv,
):
    cols, per_device, half, cols_here = left_all.shape
    rows_here = left.shape[1]
    grp, row, col = lax.axis_index("grp"), lax.axis_index("row"), lax.axis_index("col")
    inner = lax.axis_size("row") // 4
    plane = row // inner
    place = lax.rem(row, inner) * cols + col
    is_middle = (plane == 1) | (plane == 2)
    upper = plane // 2
    middle = 1 + upper
    chunk = per_device // parts

    def device(to_plane, to_place):
        return (grp, to_plane * inner + to_place // cols, lax.rem(to_place, cols))

    def row_offset(at_plane, at_row):
        return pl.multiple_of((lax.rem(at_plane, 2) * inner + at_row) * rows_here, rows_here)

    me = row * cols + col
    total = 4 * groups
    barrier = pltpu.get_barrier_semaphore()

    @pl.loop(1, total)
    def _(step):
        to = lax.rem(me + step, total)
        pl.semaphore_signal(
            barrier, inc=1, device_id=(grp, to // cols, lax.rem(to, cols)),
            device_id_type=pl.DeviceIdType.MESH,
        )

    pl.semaphore_wait(barrier, total - 1)

    my_offset = row_offset(plane, lax.rem(row, inner))

    @pl.loop(0, parts)
    def _(part):
        order = ((right, right_all, 1), (left, left_all, 0))
        for source, target, side in order:
            for step in range(groups):
                to = lax.rem(place + step, groups)
                src = source.at[pl.ds(to * per_device + part * chunk, chunk)]
                dst = target.at[col, pl.ds(part * chunk, chunk), pl.ds(my_offset, rows_here)]

                def send(src=src, dst=dst, to=to, side=side):
                    pltpu.make_async_remote_copy(
                        src_ref=src, dst_ref=dst, send_sem=send_sem.at[side, part],
                        recv_sem=side_sem.at[side, part], device_id=device(plane, to),
                        device_id_type=pl.DeviceIdType.MESH,
                    ).start()

                def keep(src=src, dst=dst, side=side):
                    pltpu.make_async_copy(src, dst, side_sem.at[side, part]).start()

                if step == 0:
                    keep()
                else:
                    send()

    def landed_side(ref, side, part):
        span = ref.at[:, pl.ds(part * chunk, chunk)]
        pltpu.make_async_copy(span, span, side_sem.at[side, part]).wait()

    plane_rows = pl.ds(
        pl.multiple_of(lax.rem(plane, 2) * inner * rows_here, rows_here), inner * rows_here
    )

    def forward(ref, side, part):
        span = ref.at[:, pl.ds(part * chunk, chunk), plane_rows]
        return pltpu.make_async_remote_copy(
            src_ref=span, dst_ref=span, send_sem=edge_send.at[side, part],
            recv_sem=side_sem.at[side, part], device_id=device(middle, place),
            device_id_type=pl.DeviceIdType.MESH,
        )

    @pl.when(jnp.logical_not(is_middle))
    def _():
        @pl.loop(0, parts)
        def _(part):
            for ref, side in ((right_all, 1), (left_all, 0)):
                span = ref.at[:, pl.ds(part * chunk, chunk), plane_rows]
                pltpu.make_async_copy(span, span, side_sem.at[side, part]).wait()
                forward(ref, side, part).start()

    leaving = right_all if outgoing else away

    def across(part):
        span = pl.ds(part * chunk, chunk)
        return pltpu.make_async_remote_copy(
            src_ref=leaving.at[:, span], dst_ref=landed.at[:, span],
            send_sem=away_send.at[part], recv_sem=away_recv.at[part],
            device_id=device(3 - middle, place), device_id_type=pl.DeviceIdType.MESH,
        )

    def begin(part):
        landed_side(right_all, 1, part)
        if not outgoing:
            landed_side(left_all, 0, part)

            @pl.loop(0, chunk)
            def _(index):
                channel = part * chunk + index
                ours = left_all[1 - upper, channel]
                for c in range(cols):
                    away[c, channel] = dot(
                        ours, right_all[c, channel], ((0,), (0,))
                    ).astype(jnp.bfloat16)

        across(part).start()

    def finish(part):
        if outgoing:
            landed_side(left_all, 0, part)
        across(part).wait_recv()

        @pl.loop(0, chunk)
        def _(index):
            channel = part * chunk + index
            if outgoing:
                for held, half_index in ((right_all, upper), (landed, 1 - upper)):
                    value = dot(left_all[0, channel], held[0, channel], ((1,), (1,)))
                    for c in range(1, cols):
                        value += dot(left_all[c, channel], held[c, channel], ((1,), (1,)))
                    result[half_index, channel] = value.astype(jnp.bfloat16)
            else:
                ours = left_all[upper, channel]
                for c in range(cols):
                    value = dot(ours, right_all[c, channel], ((0,), (0,)))
                    value += landed[c, channel].astype(jnp.float32)
                    result[c, channel] = value.astype(jnp.bfloat16)

        for edge in (True, False):
            to_plane = 3 * upper if edge else middle
            for step in range(groups):
                to = lax.rem(place + step, groups)
                offset = row_offset(to_plane, to // cols)
                src = result.at[
                    lax.rem(to, cols), pl.ds(part * chunk, chunk), pl.ds(offset, rows_here)
                ]
                dst = mixed.at[pl.ds(place * per_device + part * chunk, chunk)]
                if step == 0 and not edge:
                    pltpu.make_async_copy(src, dst, back_recv).start()
                else:
                    pltpu.make_async_remote_copy(
                        src_ref=src, dst_ref=dst, send_sem=back_send.at[part],
                        recv_sem=back_recv, device_id=device(to_plane, to),
                        device_id_type=pl.DeviceIdType.MESH,
                    ).start()

    @pl.when(is_middle)
    def _():
        begin(0)

        @pl.loop(1, parts)
        def _(part):
            begin(part)
            finish(part - 1)

        finish(parts - 1)

        @pl.loop(0, parts)
        def _(part):
            across(part).wait_send()
            sent = mixed.at[pl.ds(0, (2 * groups - 1) * chunk)]
            pltpu.make_async_copy(sent, sent, back_send.at[part]).wait()

    @pl.loop(0, parts)
    def _(part):
        for side in range(2):
            sent = left.at[pl.ds(0, (groups - 1) * chunk)]
            pltpu.make_async_copy(sent, sent, send_sem.at[side, part]).wait()

    @pl.when(jnp.logical_not(is_middle))
    def _():
        @pl.loop(0, parts)
        def _(part):
            for ref, side in ((right_all, 1), (left_all, 0)):
                forward(ref, side, part).wait_send()

    pltpu.make_async_copy(mixed, mixed, back_recv).wait()


def triangle(left, right, outgoing):
    hidden, rows_here, cols_here = left.shape
    row_count = lax.axis_size("row")
    col_count = lax.axis_size("col")
    groups = row_count // 4 * col_count
    per_device = hidden // groups
    parts = min(32, per_device)
    half = row_count // 2 * rows_here
    held = pltpu.VMEM((col_count, per_device, half, cols_here), jnp.bfloat16)
    small = pltpu.VMEM((16, 128), jnp.bfloat16)
    anywhere = pl.BlockSpec(memory_space=pl.ANY)
    sems = pltpu.SemaphoreType.DMA
    return pl.pallas_call(
        functools.partial(triangle_kernel, outgoing, groups, parts),
        in_specs=[anywhere, anywhere],
        out_specs=anywhere,
        out_shape=jax.ShapeDtypeStruct(left.shape, jnp.bfloat16),
        scratch_shapes=[
            held, held, small if outgoing else held, held, held,
            sems((2, parts)), sems((2, parts)), sems((2, parts)), sems((parts,)), sems((parts,)), sems((parts,)), sems,
        ],
        compiler_params=pltpu.CompilerParams(
            collective_id=1 if outgoing else 2, has_side_effects=True,
            vmem_limit_bytes=VMEM_LIMIT,
        ),
        name="outgoing_product" if outgoing else "incoming_product",
    )(left, right)


def body(
    pair, token_count, chain_ids, chain_term, in_gain, in_bias, proj, gate_w, hid_gain,
    hid_bias, out_w,
):
    rows_here, cols_here, width = pair.shape
    hidden = proj.shape[2] // 4
    row_first = lax.axis_index("row") * rows_here
    col_first = lax.axis_index("col") * cols_here
    positions = jnp.arange(chain_ids.shape[0], dtype=jnp.int32)
    real = (positions < token_count[0]).astype(jnp.float32)
    row_real = lax.dynamic_slice_in_dim(real, row_first, rows_here, 0)
    col_real = lax.dynamic_slice_in_dim(real, col_first, cols_here, 0)[None, :]
    row_chain = lax.dynamic_slice_in_dim(chain_ids, row_first, rows_here, 0)
    col_chain = lax.dynamic_slice_in_dim(chain_ids, col_first, cols_here, 0)[:, None]
    chain_term = chain_term[None, :]
    proj_t = proj.transpose(0, 2, 1)
    hid_gain = hid_gain[:, :, None]
    hid_bias = hid_bias[:, :, None]

    tile = 16
    smem = pl.BlockSpec(memory_space=pltpu.SMEM)
    whole = pl.BlockSpec(memory_space=pltpu.VMEM)
    pixels = pl.BlockSpec((tile, cols_here, width), lambda i: (i, 0, 0))
    planes = pl.BlockSpec((hidden, tile, cols_here), lambda i: (0, i, 0))
    planes_shape = jax.ShapeDtypeStruct((hidden, rows_here, cols_here), jnp.bfloat16)
    pixels_shape = jax.ShapeDtypeStruct(pair.shape, jnp.float32)
    rows_scratch = pltpu.VMEM((tile, hidden, cols_here), jnp.bfloat16)
    grid = (rows_here // tile,)
    params = pltpu.CompilerParams(vmem_limit_bytes=VMEM_LIMIT)

    left, right = pl.pallas_call(
        first_kernel,
        grid=grid,
        in_specs=[smem, smem, pixels] + [whole] * 6,
        out_specs=[planes, planes],
        out_shape=[planes_shape, planes_shape],
        scratch_shapes=[rows_scratch] * 2,
        compiler_params=params,
        name="first_projection",
    )(row_chain, row_real, pair, col_chain, col_real, chain_term, in_gain, in_bias, proj_t[0])
    mixed = triangle(left, right, True)
    state, left, right = pl.pallas_call(
        middle_kernel,
        grid=grid,
        in_specs=[smem, smem, pixels, planes] + [whole] * 10,
        out_specs=[pixels, planes, planes],
        out_shape=[pixels_shape, planes_shape, planes_shape],
        scratch_shapes=[rows_scratch] * 3,
        compiler_params=params,
        name="update_and_projection",
    )(
        row_chain, row_real, pair, mixed, col_chain, col_real, chain_term, in_gain, in_bias,
        proj_t[1], gate_w[0], hid_gain[0], hid_bias[0], out_w[0],
    )
    mixed = triangle(left, right, False)
    return pl.pallas_call(
        last_kernel,
        grid=grid,
        in_specs=[pixels, planes] + [whole] * 6,
        out_specs=pixels,
        out_shape=pixels_shape,
        scratch_shapes=[rows_scratch],
        compiler_params=params,
        name="last_update",
    )(state, mixed, in_gain, in_bias, gate_w[1], hid_gain[1], hid_bias[1], out_w[1])


def solution(mesh):
    return jax.shard_map(
        body,
        mesh=mesh,
        in_specs=(P(("grp", "row"), "col", None), P("grp"), P("grp")) + (P(),) * 8,
        out_specs=P(("grp", "row"), "col", None),
        check_vma=False,
    )
```
